512 devices in a mesh: gx: 32 (over x, z), gy: 16 (over y, core).
Axes of the slice: x: 4, y: 8, z: 8, core: 2. Of those that a mesh axis runs over, the one named last changes fastest.
Arguments:
- features: bfloat16 [96, 2097152], P(None, ('gx', 'gy')), may hold values from -6 to 6
- kernel_map: int32 [27, 2097152], P(None, ('gx', 'gy')), may hold values from 0 to 13312, as said below
- send_rows: int32 [524288], P(('gx', 'gy')), may hold values from 0 to 4095
- conv_weight: bfloat16 [27, 96, 96], replicated, may hold values from -0.15625 to 0.15625
- conv_gain: float32 [96], replicated, may hold values from 0.5 to 1.5
- conv_bias: float32 [96], replicated, may hold values from -2 to 2
- down_weight: bfloat16 [8, 192, 96], replicated, may hold values from -0.3125 to 0.3125
- coarse_dest: int32 [512], P(('gx', 'gy')), may hold values from 0 to 3, as said below
Outputs:
- fine_out: bfloat16 [96, 2097152], P(None, ('gx', 'gy'))
- coarse_out: bfloat16 [192, 262144], P(None, ('gx', 'gy'))
The draws below stay inside these ranges and needn't reach their ends.
Inputs may be any that keep to these rules, and one draw needn't show every extreme that they name: kernel_map[13, q] is q's own slot within its device where q is occupied and 13312 elsewhere; the value 4096 + 9 * 1024 means no input. c = coarse_dest[b] always names a device on the mesh as described in the reference program.
All inputs are finite; a program needn't handle non-finite values.
Results may differ from the reference program's by a relative error of at most 0.0095.
Values may be sent and summed in bfloat16 or wider, within the bound.
A program may use at most 64 MiB of HBM per device.

```python
import jax
import jax.numpy as jnp
from jax import lax

C1 = 96
C2 = 192
BLK = 4096
KOFF = 27
NB = 1
BND = 1024
SITES = 2097152
BLOCKS = 512
CB = 512
N_GX = 32
N_GY = 16


def draw_kernel_map(key, part):
    slots_dev = NB * BLK
    total_slots = slots_dev * N_GX * N_GY
    device = jnp.arange(total_slots, dtype=jnp.int32) // slots_dev
    key_occ, key_act, key_kind, key_own, key_tile, key_row = jax.random.split(key, 6)
    occupancy = jax.random.randint(key_occ, (N_GX * N_GY,), 30, 96)
    active = jax.random.randint(key_act, (total_slots,), 0, 100) < occupancy[device]
    kinds = jax.random.randint(key_kind, (KOFF, total_slots), 0, 10)
    own_slot = jax.random.randint(key_own, (KOFF, total_slots), 0, slots_dev)
    tile_num = jax.random.randint(key_tile, (KOFF, total_slots), 0, 8)
    tile_num = tile_num + (tile_num >= 4).astype(jnp.int32)
    row_num = jax.random.randint(key_row, (KOFF, total_slots), 0, BND)
    empty = slots_dev + 9 * BND
    values = jnp.where(kinds < 4, own_slot, jnp.where(kinds < 7, slots_dev + tile_num * BND + row_num, empty))
    local_slot = jnp.arange(total_slots, dtype=jnp.int32) % slots_dev
    centre = (jnp.arange(KOFF, dtype=jnp.int32) == KOFF // 2)[:, None]
    values = jnp.where(centre, local_slot[None, :], values)
    return jnp.where(active[None, :], values, empty).astype(jnp.int32)


def draw_coarse_dest(key, part):
    total_blocks = NB * N_GX * N_GY
    device = jnp.arange(total_blocks, dtype=jnp.int32) // NB
    key_x, key_y, key_sub = jax.random.split(key, 3)
    step_x = jax.random.randint(key_x, (total_blocks,), 0, 2) * (device // N_GY > 0).astype(jnp.int32)
    step_y = jax.random.randint(key_y, (total_blocks,), 0, 2) * (device % N_GY > 0).astype(jnp.int32)
    sub_block = jax.random.randint(key_sub, (total_blocks,), 0, NB)
    return ((step_x + 2 * step_y) * NB + sub_block).astype(jnp.int32)


def place_ends(result, key, least, largest):
    index_at = [jax.random.randint(jax.random.fold_in(key, axis), (), 0, length) for axis, length in enumerate(result.shape)]
    longest = result.shape.index(max(result.shape))
    next_to = index_at[:longest] + [(index_at[longest] + 1) % result.shape[longest]] + index_at[longest + 1:]
    return result.at[tuple(index_at)].set(least).at[tuple(next_to)].set(largest)


def steps_of(own_key, extent, pieces, smallest, largest):
    gain, own = 1.0, jax.random.fold_in(own_key, 6)
    for position, parts in pieces:
        heights = jnp.exp(jax.random.uniform(jax.random.fold_in(own, position), (parts,), jnp.float32, smallest / len(pieces), largest / len(pieces)))
        gain = gain * jnp.repeat(heights, extent[position] // parts).reshape([-1 if axis == position else 1 for axis in range(len(extent))])
    return gain


def centred(key, extent, width, most, cuts=(), held_as=jnp.bfloat16):
    result = jax.random.normal(key, extent, jnp.float32) * width
    if len(cuts) > 0:
        result = steps_of(key, extent, cuts, -0.22, 0.18) * result
    return jnp.clip(result, min=-most, max=most).astype(held_as)


def setup_inputs(seed: int = 0) -> dict:
    key_list = jax.random.split(jax.random.key(seed), 9)
    return {
        "features": centred(key_list[0], (C1, SITES), 1.0, 6.0, ((1, 512),)),
        "kernel_map": draw_kernel_map(jax.random.fold_in(key_list[8], 71), 0),
        "send_rows": place_ends(jax.random.randint(key_list[2], (BND * N_GX * N_GY,), 0, NB * BLK), jax.random.fold_in(key_list[2], 1), 0, (NB * BLK) - 1).astype(jnp.int32),
        "conv_weight": centred(key_list[3], (KOFF, C1, C1), (KOFF * C1 * 6 // 10) ** -0.5, 0.15625),
        "conv_gain": jnp.clip(1.0 + 0.1 * jax.random.normal(key_list[4], (C1,), jnp.float32), 0.5, 1.5),
        "conv_bias": centred(key_list[5], (C1,), 0.5, 2.0, (), jnp.float32),
        "down_weight": centred(key_list[6], (8, C2, C1), (4 * C1) ** -0.5, 0.3125),
        "coarse_dest": draw_coarse_dest(jax.random.fold_in(key_list[8], 71), 0),
    }


def resolve_slots(index, send_rows):
    slots_dev = NB * BLK
    columns = jnp.arange(SITES, dtype=jnp.int32)
    device = columns // slots_dev
    gx_pos = device // N_GY
    gy_pos = device % N_GY
    relative = jnp.clip(index - slots_dev, 0, 9 * BND - 1)
    tile_num = relative // BND
    row_num = relative % BND
    near_x = gx_pos + tile_num // 3 - 1
    near_y = gy_pos + tile_num % 3 - 1
    inside = (near_x >= 0) & (near_x < N_GX) & (near_y >= 0) & (near_y < N_GY)
    peer = jnp.clip(near_x, 0, N_GX - 1) * N_GY + jnp.clip(near_y, 0, N_GY - 1)
    remote = peer * slots_dev + send_rows[peer * BND + row_num]
    own_slot = index < slots_dev
    halo_ok = (index >= slots_dev) & (index < slots_dev + 9 * BND) & inside
    source = jnp.where(own_slot, device * slots_dev + index, remote)
    return jnp.where(own_slot | halo_ok, source, SITES).astype(jnp.int32)


def reference(features, kernel_map, send_rows, conv_weight, conv_gain, conv_bias, down_weight, coarse_dest):
    def add_offset(totals, offset):
        source = resolve_slots(kernel_map[offset], send_rows)
        gathered = jnp.take(features, source, axis=1, mode="fill", fill_value=0)
        return totals + jnp.dot(conv_weight[offset], gathered, preferred_element_type=jnp.float32), None

    totals, _ = lax.scan(add_offset, jnp.zeros((C1, SITES), jnp.float32), jnp.arange(KOFF, dtype=jnp.int32))
    active = (kernel_map[KOFF // 2] < NB * BLK).astype(jnp.float32)
    fine_out = (jax.nn.relu(totals * conv_gain[:, None] + conv_bias[:, None]) * active[None, :]).astype(jnp.bfloat16)
    planes = fine_out.astype(jnp.float32).reshape(C1, BLOCKS, 8, CB)
    partial_value = jnp.einsum("pod,dbpv->bov", down_weight.astype(jnp.float32), planes)
    block_ids = jnp.arange(BLOCKS, dtype=jnp.int32)
    device = block_ids // NB
    owner_class = coarse_dest // NB
    owner = (device // N_GY - owner_class % 2) * N_GY + (device % N_GY - owner_class // 2)
    target = (owner * NB + coarse_dest % NB).astype(jnp.int32)
    summed = jax.ops.segment_sum(partial_value, target, num_segments=BLOCKS)
    coarse_out = jnp.transpose(summed, (1, 0, 2)).reshape(C2, BLOCKS * CB).astype(jnp.bfloat16)
    return fine_out, coarse_out
```

```python
import jax
import jax.numpy as jnp
from jax import lax
from jax.experimental import pallas as pl
from jax.experimental.pallas import tpu as pltpu
from jax.sharding import PartitionSpec as P

F32 = jnp.float32
BF16 = jnp.bfloat16
LANES = 128
QC = 512


def padded(shard, sides, width):
    for axis, dim in sides:
        devices, length = (lax.axis_size(axis), shard.shape[dim])
        up = [(i, (i + 1) % devices) for i in range(devices - 1)]
        down = [(j, i) for i, j in up]
        last = lax.slice_in_dim(shard, length - width, length, axis=dim)
        leading = lax.slice_in_dim(shard, 0, width, axis=dim)
        before = lax.ppermute(last, axis, up)
        after = lax.ppermute(leading, axis, down)
        shard = jnp.concatenate([before, shard, after], axis=dim)
    return shard


def passed_along(shard, axis, by):
    devices = lax.axis_size(axis)
    pairs = [(i, i + by) for i in range(devices) if 0 <= i + by < devices]
    return lax.ppermute(shard, axis, pairs)


def dot_nt(a, b):
    return lax.dot_general(a, b, (((1,), (1,)), ((), ())), preferred_element_type=F32)


def conv_kernel(
    map_ref, feat_ref, halo_ref, w_ref, gain_ref, bias_ref, down_ref,
    fine_ref, part_ref,
    idx_a, idx_b, tiles, table, wpair, acc, sems, ga0, ga1, gb0, gb1,
):
    channels, slots = feat_ref.shape
    halo_len = halo_ref.shape[1]
    koff = map_ref.shape[0]
    centre = koff // 2
    others = [k for k in range(koff) if k != centre]
    pairs = len(others) // 2
    blocks = slots // QC
    total = blocks * pairs
    lane_tiles = QC // LANES
    idx = (idx_a, idx_b)
    rows = ((ga0, ga1), (gb0, gb1))

    wpair[...] = jnp.zeros_like(wpair)
    for n, k in enumerate(others):
        wpair[n // 2, :, pl.ds((n % 2) * LANES, channels)] = w_ref[k]

    for b in range(blocks):
        for j in range(pairs):
            for h in range(2):
                for t in range(lane_tiles):
                    tiles[b * pairs + j, pl.ds(h * lane_tiles + t, 1), :] = map_ref[
                        pl.ds(others[2 * j + h], 1), pl.ds(b * QC + t * LANES, LANES)
                    ]

    step = 256
    eye = (
        lax.broadcasted_iota(jnp.int32, (step, step), 0)
        == lax.broadcasted_iota(jnp.int32, (step, step), 1)
    ).astype(BF16)
    pad = jnp.zeros((LANES - channels, step), BF16)

    def transpose_in(src, base, count):
        def one(i, _):
            c0 = pl.multiple_of(i * step, step)
            x = jnp.concatenate([src[:, pl.ds(c0, step)], pad], axis=0)
            table[pl.ds(pl.multiple_of(base + c0, step), step), :] = dot_nt(eye, x)
            return 0

        lax.fori_loop(0, count // step, one, 0)

    transpose_in(feat_ref, 0, slots)
    transpose_in(halo_ref, slots, halo_len)
    table[pl.ds(slots + halo_len, 8), :] = jnp.zeros((8, LANES), F32)

    def fetch(t, s):
        return pltpu.make_async_copy(tiles.at[t], idx[s], sems.at[s])

    def gather(s):
        for h in range(2):
            for r in range(QC):
                at = idx[s][h * lane_tiles + r // LANES, r % LANES]
                rows[s][h][pl.ds(r, 1), :] = table[pl.ds(at, 1), :]

    def multiply(t, s):
        j = lax.rem(t, pairs)
        g = jnp.concatenate([rows[s][0][...], rows[s][1][...]], axis=1).astype(BF16)
        keep = jnp.where(j == 0, 0.0, 1.0)
        acc[...] = acc[...] * keep + dot_nt(wpair[j], g)

    def finish(t):
        b = lax.div(t, pairs)

        @pl.when(t - b * pairs == pairs - 1)
        def _():
            cols = pl.ds(pl.multiple_of(b * QC, QC), QC)
            conv = acc[...] + jnp.dot(
                w_ref[centre], feat_ref[:, cols], preferred_element_type=F32
            )
            active = (map_ref[centre : centre + 1, cols] < slots).astype(F32)
            fine = jnp.maximum(conv * gain_ref[...] + bias_ref[...], 0.0) * active
            fine = fine.astype(BF16)
            fine_ref[:, cols] = fine
            prior = jnp.where(b == 0, 0.0, 1.0)
            part_ref[...] = part_ref[...] * prior + jnp.dot(
                down_ref[b], fine, preferred_element_type=F32
            )

    acc[...] = jnp.zeros_like(acc)
    part_ref[...] = jnp.zeros_like(part_ref)
    fetch(0, 0).start()
    fetch(1, 1).start()
    fetch(0, 0).wait()
    gather(0)
    fetch(2, 0).start()

    def body(i, _):
        for s in (1, 0):
            t = 2 * i + (1 if s == 1 else 2)
            fetch(t, s).wait()
            multiply(t - 1, 1 - s)
            gather(s)
            fetch(jnp.minimum(t + 2, total - 1), s).start()
            finish(t - 1)
        return 0

    lax.fori_loop(0, (total - 2) // 2, body, 0)
    fetch(total - 1, 1).wait()
    multiply(total - 2, 0)
    gather(1)
    finish(total - 2)
    multiply(total - 1, 1)
    finish(total - 1)
    fetch(total - 1, 0).wait()


def conv_call(kernel_map, features, halo, conv_weight, gain, bias, down_weight):
    channels, slots = features.shape
    koff = kernel_map.shape[0]
    pairs = koff // 2
    total = slots // QC * pairs
    out_channels = down_weight.shape[1]
    vmem = pl.BlockSpec(memory_space=pltpu.VMEM)
    return pl.pallas_call(
        conv_kernel,
        in_specs=[vmem] * 7,
        out_specs=[vmem] * 2,
        out_shape=[
            jax.ShapeDtypeStruct((channels, slots), BF16),
            jax.ShapeDtypeStruct((out_channels, slots // 8), F32),
        ],
        scratch_shapes=[
            pltpu.SMEM((8, LANES), jnp.int32),
            pltpu.SMEM((8, LANES), jnp.int32),
            pltpu.VMEM((total, 8, LANES), jnp.int32),
            pltpu.VMEM((slots + halo.shape[1] + 8, LANES), F32),
            pltpu.VMEM((pairs, channels, 2 * LANES), BF16),
            pltpu.VMEM((channels, QC), F32),
            pltpu.SemaphoreType.DMA((2,)),
        ]
        + [pltpu.VMEM((QC, LANES), F32)] * 4,
        compiler_params=pltpu.CompilerParams(vmem_limit_bytes=48 * 2**20),
        name="conv",
    )(kernel_map, features, halo, conv_weight, gain, bias, down_weight)


def shards(
    features, kernel_map, send_rows, conv_weight, conv_gain, conv_bias, down_weight, coarse_dest
):
    channels, slots_dev = features.shape
    boundary_len = send_rows.shape[0]
    feature_rows = jnp.transpose(features)
    boundary = jnp.take(feature_rows, send_rows, axis=0)
    boundary = jnp.transpose(boundary).reshape(channels, 1, 1, boundary_len)
    halo = padded(boundary, (("gx", 1), ("gy", 2)), 1).reshape(channels, 9 * boundary_len)
    fine_out, partial = conv_call(
        kernel_map, features, halo, conv_weight, conv_gain[:, None], conv_bias[:, None], down_weight
    )
    dest = coarse_dest[0]
    routed = [jnp.where(dest == c, partial, 0.0) for c in range(4)]
    from_x = passed_along(routed[1].astype(BF16), "gx", -1).astype(F32)
    from_y = passed_along(routed[2].astype(BF16), "gy", -1).astype(F32)
    corner = passed_along(routed[3].astype(BF16), "gx", -1)
    from_corner = passed_along(corner, "gy", -1).astype(F32)
    coarse_out = (routed[0] + from_x + from_y + from_corner).astype(BF16)
    return (fine_out, coarse_out)


def solution(mesh):
    placed = (
        P(None, ("gx", "gy")),
        P(None, ("gx", "gy")),
        P(("gx", "gy")),
        P(),
        P(),
        P(),
        P(),
        P(("gx", "gy")),
    )
    return jax.shard_map(
        shards,
        mesh=mesh,
        in_specs=placed,
        out_specs=(P(None, ("gx", "gy")), P(None, ("gx", "gy"))),
        check_vma=False,
    )
```

```python
import jax
import jax.numpy as jnp
from jax import lax
from jax.experimental import pallas as pl
from jax.experimental.pallas import tpu as pltpu
from jax.sharding import PartitionSpec as P

F32 = jnp.float32
BF16 = jnp.bfloat16
LANES = 128
QC = 512
PARTS = 2
MESH = pl.DeviceIdType.MESH


def dot_nt(a, b):
    return lax.dot_general(a, b, (((1,), (1,)), ((), ())), preferred_element_type=F32)


def eye(rows, cols):
    r = lax.broadcasted_iota(jnp.int32, (rows, cols), 0)
    c = lax.broadcasted_iota(jnp.int32, (rows, cols), 1)
    return (r == c).astype(BF16)


def conv_kernel(
    nx, ny,
    send_ref, dest_ref, map_ref, feat_ref, w_ref, gain_ref, bias_ref, down_ref,
    fine_ref, coarse_ref,
    idx_a, idx_b, tiles, table, offered, halo, wpair, acc, part, out_x, in_x, out_y, in_y,
    idx_sem, halo_send, halo_recv, x_send, x_recv, y_send, y_recv,
    ga0, ga1, gb0, gb1,
):
    channels, slots = feat_ref.shape
    bnd = halo.shape[2]
    koff = map_ref.shape[0]
    centre = koff // 2
    others = [k for k in range(koff) if k != centre]
    pairs = len(others) // 2
    blocks = slots // QC
    total = blocks * pairs
    lane_tiles = QC // LANES
    coarse_len = slots // 8
    halves = 8 // lane_tiles
    chunks = blocks // halves
    out_channels = part.shape[1]
    idx = (idx_a, idx_b)
    rows = ((ga0, ga1), (gb0, gb1))

    i, j = lax.axis_index("gx"), lax.axis_index("gy")
    has_left, has_right = i > 0, i < nx - 1
    has_down, has_up = j > 0, j < ny - 1
    around = (
        (has_left, (i - 1, j)),
        (has_right, (i + 1, j)),
        (has_down, (i, j - 1)),
        (has_up, (i, j + 1)),
    )

    halo[...] = jnp.zeros_like(halo)
    in_x[...] = jnp.zeros_like(in_x)
    in_y[...] = jnp.zeros_like(in_y)

    barrier = pltpu.get_barrier_semaphore()
    for there, device in around:
        @pl.when(there)
        def _():
            pl.semaphore_signal(barrier, inc=1, device_id=device, device_id_type=MESH)

    step = 256
    ident = eye(step, step)
    pad = jnp.zeros((LANES - channels, step), BF16)

    def own_rows(n, _):
        c0 = pl.multiple_of(n * step, step)
        x = jnp.concatenate([feat_ref[:, pl.ds(c0, step)], pad], axis=0)
        table[pl.ds(c0, step), :] = dot_nt(ident, x)
        return 0

    lax.fori_loop(0, slots // step, own_rows, 0, unroll=2)
    table[pl.ds(slots + 9 * bnd, 8), :] = jnp.zeros((8, LANES), F32)

    for r in range(bnd):
        offered[pl.ds(r, 1), :] = table[pl.ds(send_ref[r], 1), :]
    halo[4] = dot_nt(eye(channels, LANES), offered[...].astype(BF16)).astype(BF16)

    pl.semaphore_wait(barrier, sum(there.astype(jnp.int32) for there, _ in around))

    right, left, up, down = (i + 1, j), (i - 1, j), (i, j + 1), (i, j - 1)
    both = jnp.logical_and
    sends = (
        (4, 1, right, has_right, has_left),
        (4, 7, left, has_left, has_right),
        (4, 3, up, has_up, has_down),
        (4, 5, down, has_down, has_up),
        (1, 0, up, both(has_left, has_up), both(has_left, has_down)),
        (1, 2, down, both(has_left, has_down), both(has_left, has_up)),
        (7, 6, up, both(has_right, has_up), both(has_right, has_down)),
        (7, 8, down, both(has_right, has_down), both(has_right, has_up)),
    )
    depth = channels // PARTS

    def boundary(n, piece):
        src, dst, device, _, _ = sends[n]
        span = pl.ds(piece * depth, depth)
        return pltpu.make_async_remote_copy(
            src_ref=halo.at[src, span],
            dst_ref=halo.at[dst, span],
            send_sem=halo_send.at[n, piece],
            recv_sem=halo_recv.at[n, piece],
            device_id=device,
            device_id_type=MESH,
        )

    def start(n, piece):
        @pl.when(sends[n][3])
        def _():
            boundary(n, piece).start()

    def arrived(n, piece):
        @pl.when(sends[n][4])
        def _():
            boundary(n, piece).wait_recv()

    for piece in range(PARTS):
        for n in range(4):
            start(n, piece)

    wpair[...] = jnp.zeros_like(wpair)
    for n, k in enumerate(others):
        wpair[n // 2, :, pl.ds((n % 2) * LANES, channels)] = w_ref[k]

    def first_col(b, t):
        return ((b % halves) * lane_tiles + t) * coarse_len + (b // halves) * LANES

    for b in range(blocks):
        for m in range(pairs):
            for h in range(2):
                for t in range(lane_tiles):
                    tiles[b * pairs + m, pl.ds(h * lane_tiles + t, 1), :] = map_ref[
                        pl.ds(others[2 * m + h], 1), pl.ds(first_col(b, t), LANES)
                    ]

    def tile_rows(t):
        for n in range(bnd // step):
            x = jnp.concatenate([halo[t, :, pl.ds(n * step, step)], pad], axis=0)
            table[pl.ds(slots + t * bnd + n * step, step), :] = dot_nt(ident, x)

    tile_rows(4)
    for piece in range(PARTS):
        arrived(0, piece)
        start(4, piece)
        start(5, piece)
        arrived(1, piece)
        start(6, piece)
        start(7, piece)
    tile_rows(1)
    tile_rows(7)
    for n in range(2, 8):
        for piece in range(PARTS):
            arrived(n, piece)
        tile_rows(sends[n][1])

    def fetch(t, s):
        return pltpu.make_async_copy(tiles.at[t], idx[s], idx_sem.at[s])

    def gather(s):
        for h in range(2):
            for r in range(QC):
                at = idx[s][h * lane_tiles + r // LANES, r % LANES]
                rows[s][h][pl.ds(r, 1), :] = table[pl.ds(at, 1), :]

    def multiply(t, s):
        m = lax.rem(t, pairs)
        g = jnp.concatenate([rows[s][0][...], rows[s][1][...]], axis=1).astype(BF16)
        keep = jnp.where(m == 0, 0.0, 1.0)
        acc[...] = acc[...] * keep + dot_nt(wpair[m], g)

    dest = dest_ref[0]
    out_x[:, pl.ds(out_channels, 16), :] = jnp.full(
        (chunks, 16, LANES), dest.astype(F32), F32
    ).astype(BF16)

    def to_left(v):
        return pltpu.make_async_remote_copy(
            src_ref=out_x.at[v], dst_ref=in_x.at[v],
            send_sem=x_send.at[v], recv_sem=x_recv.at[v],
            device_id=left, device_id_type=MESH,
        )

    def to_down(v):
        return pltpu.make_async_remote_copy(
            src_ref=out_y.at[v], dst_ref=in_y.at[v],
            send_sem=y_send.at[v], recv_sem=y_recv.at[v],
            device_id=down, device_id_type=MESH,
        )

    def from_right(v, which):
        got = in_x[v].astype(F32)
        kind = got[out_channels : out_channels + 1]
        return jnp.where(kind == float(which), got[:out_channels], 0.0)

    def finish(t):
        b = lax.div(t, pairs)

        @pl.when(t - b * pairs == pairs - 1)
        def _():
            v = lax.div(b, halves)
            half = b - v * halves
            new = jnp.zeros((out_channels, LANES), F32)
            for u in range(lane_tiles):
                p = half * lane_tiles + u
                cols = pl.ds(pl.multiple_of(p * coarse_len + v * LANES, LANES), LANES)
                conv = acc[:, u * LANES : (u + 1) * LANES] + jnp.dot(
                    w_ref[centre], feat_ref[:, cols], preferred_element_type=F32
                )
                active = (map_ref[centre : centre + 1, cols] < slots).astype(F32)
                fine = jnp.maximum(conv * gain_ref[...] + bias_ref[...], 0.0) * active
                fine = fine.astype(BF16)
                fine_ref[:, cols] = fine
                new = new + jnp.dot(down_ref[p], fine, preferred_element_type=F32)
            part[v] = part[v] + new

            @pl.when(half == halves - 1)
            def _():
                out_x[v, pl.ds(0, out_channels), :] = part[v].astype(BF16)

                @pl.when(has_left)
                def _():
                    to_left(v).start()

    def onwards(v):
        @pl.when(has_right)
        def _():
            to_left(v).wait_recv()

        out_y[v] = (jnp.where(dest == 2, part[v], 0.0) + from_right(v, 3)).astype(BF16)

        @pl.when(has_down)
        def _():
            to_down(v).start()

    part[...] = jnp.zeros_like(part)
    acc[...] = jnp.zeros_like(acc)
    fetch(0, 0).start()
    fetch(1, 1).start()
    fetch(0, 0).wait()
    gather(0)
    fetch(2, 0).start()

    def body(n, _):
        for s in (1, 0):
            t = 2 * n + (1 if s == 1 else 2)
            fetch(t, s).wait()
            multiply(t - 1, 1 - s)
            gather(s)
            fetch(jnp.minimum(t + 2, total - 1), s).start()
            finish(t - 1)
        per_chunk = pairs * halves
        v = lax.div(2 * n, per_chunk)

        @pl.when(jnp.logical_and(v > 0, 2 * n - v * per_chunk == pairs - 1))
        def _():
            onwards(v - 1)

        return 0

    lax.fori_loop(0, (total - 2) // 2, body, 0)
    fetch(total - 1, 1).wait()
    multiply(total - 2, 0)
    gather(1)
    finish(total - 2)
    multiply(total - 1, 1)
    finish(total - 1)
    fetch(total - 1, 0).wait()

    onwards(chunks - 1)
    for v in range(chunks):
        @pl.when(has_up)
        def _():
            to_down(v).wait_recv()

        coarse_ref[:, pl.ds(v * LANES, LANES)] = (
            jnp.where(dest == 0, part[v], 0.0) + from_right(v, 1) + in_y[v].astype(F32)
        ).astype(BF16)

    for n in range(8):
        @pl.when(sends[n][3])
        def _():
            for piece in range(PARTS):
                boundary(n, piece).wait_send()
    for v in range(chunks):
        @pl.when(has_left)
        def _():
            to_left(v).wait_send()

        @pl.when(has_down)
        def _():
            to_down(v).wait_send()


def shards(
    features, kernel_map, send_rows, conv_weight, conv_gain, conv_bias, down_weight, coarse_dest
):
    channels, slots = features.shape
    bnd = send_rows.shape[0]
    koff = kernel_map.shape[0]
    pairs = koff // 2
    total = slots // QC * pairs
    out_channels = down_weight.shape[1]
    coarse_len = slots // 8
    chunks = coarse_len // LANES
    nx, ny = lax.axis_size("gx"), lax.axis_size("gy")
    vmem = pl.BlockSpec(memory_space=pltpu.VMEM)
    smem = pl.BlockSpec(memory_space=pltpu.SMEM)

    def kernel(*refs):
        conv_kernel(nx, ny, *refs)

    fine, coarse = pl.pallas_call(
        kernel,
        in_specs=[smem] * 2 + [vmem] * 6,
        out_specs=[vmem] * 2,
        out_shape=[
            jax.ShapeDtypeStruct((channels, slots), BF16),
            jax.ShapeDtypeStruct((out_channels, coarse_len), BF16),
        ],
        scratch_shapes=[
            pltpu.SMEM((8, LANES), jnp.int32),
            pltpu.SMEM((8, LANES), jnp.int32),
            pltpu.VMEM((total, 8, LANES), jnp.int32),
            pltpu.VMEM((slots + 9 * bnd + 8, LANES), F32),
            pltpu.VMEM((bnd, LANES), F32),
            pltpu.VMEM((9, channels, bnd), BF16),
            pltpu.VMEM((pairs, channels, 2 * LANES), BF16),
            pltpu.VMEM((channels, QC), F32),
            pltpu.VMEM((chunks, out_channels, LANES), F32),
            pltpu.VMEM((chunks, out_channels + 16, LANES), BF16),
            pltpu.VMEM((chunks, out_channels + 16, LANES), BF16),
            pltpu.VMEM((chunks, out_channels, LANES), BF16),
            pltpu.VMEM((chunks, out_channels, LANES), BF16),
            pltpu.SemaphoreType.DMA((2,)),
            pltpu.SemaphoreType.DMA((8, PARTS)),
            pltpu.SemaphoreType.DMA((8, PARTS)),
            pltpu.SemaphoreType.DMA((chunks,)),
            pltpu.SemaphoreType.DMA((chunks,)),
            pltpu.SemaphoreType.DMA((chunks,)),
            pltpu.SemaphoreType.DMA((chunks,)),
        ]
        + [pltpu.VMEM((QC, LANES), F32)] * 4,
        compiler_params=pltpu.CompilerParams(
            vmem_limit_bytes=48 * 2**20, collective_id=0, has_side_effects=True
        ),
        name="sparse_conv",
    )(
        send_rows, coarse_dest, kernel_map, features, conv_weight,
        conv_gain[:, None], conv_bias[:, None], down_weight,
    )
    return (fine, coarse)


def solution(mesh):
    placed = (
        P(None, ("gx", "gy")),
        P(None, ("gx", "gy")),
        P(("gx", "gy")),
        P(),
        P(),
        P(),
        P(),
        P(("gx", "gy")),
    )
    return jax.shard_map(
        shards,
        mesh=mesh,
        in_specs=placed,
        out_specs=(P(None, ("gx", "gy")), P(None, ("gx", "gy"))),
        check_vma=False,
    )
```

```python
import jax
import jax.numpy as jnp
from jax import lax
from jax.experimental import pallas as pl
from jax.experimental.pallas import tpu as pltpu
from jax.sharding import PartitionSpec as P

F32 = jnp.float32
BF16 = jnp.bfloat16
LANES = 128
QC = 1024
PARTS = 3
MESH = pl.DeviceIdType.MESH


def dot_nt(a, b):
    return lax.dot_general(a, b, (((1,), (1,)), ((), ())), preferred_element_type=F32)


def eye(rows, cols):
    r = lax.broadcasted_iota(jnp.int32, (rows, cols), 0)
    c = lax.broadcasted_iota(jnp.int32, (rows, cols), 1)
    return (r == c).astype(BF16)


def conv_kernel(
    nx, ny,
    dest_ref, *refs,
):
    hbm, refs = refs[:7], refs[7:]
    fine_ref, coarse_ref = refs[:2]
    here, in_sem = refs[2:9], refs[9]
    compute(nx, ny, dest_ref, fine_ref, coarse_ref, hbm, here, in_sem, *refs[10:])


def compute(
    nx, ny, dest_ref, fine_ref, coarse_ref, hbm, here, in_sem,
    idx_a, idx_b, tiles, table, offered, halo, wpair, acc, part, out_x, in_x, out_y, in_y,
    idx_sem, halo_send, halo_recv, x_send, x_recv, y_send, y_recv,
    gain_ref, bias_ref,
):
    send_ref, map_ref, feat_ref, w_ref, gain_row, bias_row, down_ref = here
    send_n, map_n, feat_n, w_n, gain_n, bias_n, down_n = range(7)

    def load(n):
        return pltpu.make_async_copy(hbm[n], here[n], in_sem.at[n])

    for n in (feat_n, send_n, w_n, map_n, gain_n, bias_n, down_n):
        load(n).start()
    channels, slots = feat_ref.shape
    bnd = halo.shape[2]
    koff = map_ref.shape[0]
    centre = koff // 2
    others = [k for k in range(koff) if k != centre]
    pairs = len(others) // 2
    blocks = slots // QC
    total = blocks * pairs
    lane_tiles = QC // LANES
    coarse_len = slots // 8
    halves = 8 // lane_tiles
    chunks = blocks // halves
    out_channels = part.shape[1]
    idx = (idx_a, idx_b)

    i, j = lax.axis_index("gx"), lax.axis_index("gy")
    has_left, has_right = i > 0, i < nx - 1
    has_down, has_up = j > 0, j < ny - 1
    around = (
        (has_left, (i - 1, j)),
        (has_right, (i + 1, j)),
        (has_down, (i, j - 1)),
        (has_up, (i, j + 1)),
    )

    both = jnp.logical_and
    inner = both(both(has_left, has_right), both(has_down, has_up))

    @pl.when(jnp.logical_not(inner))
    def _():
        halo[...] = jnp.zeros_like(halo)
        in_x[...] = jnp.zeros_like(in_x)
        in_y[...] = jnp.zeros_like(in_y)

    barrier = pltpu.get_barrier_semaphore()
    for there, device in around:
        @pl.when(there)
        def _():
            pl.semaphore_signal(barrier, inc=1, device_id=device, device_id_type=MESH)

    step = 256
    ident = eye(step, step)
    pad = jnp.zeros((LANES - channels, step), BF16)

    def own_rows(n, _):
        c0 = pl.multiple_of(n * step, step)
        x = jnp.concatenate([feat_ref[:, pl.ds(c0, step)], pad], axis=0)
        table[pl.ds(c0, step), :] = dot_nt(ident, x)
        return 0

    load(feat_n).wait()
    lax.fori_loop(0, slots // step, own_rows, 0, unroll=8)
    table[pl.ds(slots + 9 * bnd, 8), :] = jnp.zeros((8, LANES), F32)

    load(send_n).wait()
    for r in range(bnd):
        offered[pl.ds(r, 1), :] = table[pl.ds(send_ref[r], 1), :]
    halo[4] = dot_nt(eye(channels, LANES), offered[...].astype(BF16)).astype(BF16)

    pl.semaphore_wait(barrier, sum(there.astype(jnp.int32) for there, _ in around))

    right, left, up, down = (i + 1, j), (i - 1, j), (i, j + 1), (i, j - 1)
    sends = (
        (4, 1, right, has_right, has_left),
        (4, 7, left, has_left, has_right),
        (4, 3, up, has_up, has_down),
        (4, 5, down, has_down, has_up),
        (1, 0, up, both(has_left, has_up), both(has_left, has_down)),
        (1, 2, down, both(has_left, has_down), both(has_left, has_up)),
        (7, 6, up, both(has_right, has_up), both(has_right, has_down)),
        (7, 8, down, both(has_right, has_down), both(has_right, has_up)),
    )
    depth = channels // PARTS

    def boundary(n, piece):
        src, dst, device, _, _ = sends[n]
        span = pl.ds(piece * depth, depth)
        return pltpu.make_async_remote_copy(
            src_ref=halo.at[src, span],
            dst_ref=halo.at[dst, span],
            send_sem=halo_send.at[n, piece],
            recv_sem=halo_recv.at[n, piece],
            device_id=device,
            device_id_type=MESH,
        )

    def start(n, piece):
        @pl.when(sends[n][3])
        def _():
            boundary(n, piece).start()

    def arrived(n, piece):
        @pl.when(sends[n][4])
        def _():
            boundary(n, piece).wait_recv()

    for piece in range(PARTS):
        for n in range(4):
            start(n, piece)

    load(w_n).wait()
    wpair[...] = jnp.zeros_like(wpair)
    for n, k in enumerate(others):
        wpair[n // 2, :, pl.ds((n % 2) * LANES, channels)] = w_ref[k]

    load(gain_n).wait()
    load(bias_n).wait()
    for row, column in ((gain_row, gain_ref), (bias_row, bias_ref)):
        spread = jnp.where(eye(channels, channels) > 0, row[...], 0.0)
        column[...] = jnp.sum(spread, axis=1, keepdims=True)
    load(down_n).wait()
    load(map_n).wait()

    def first_col(b, t):
        return ((b % halves) * lane_tiles + t) * coarse_len + (b // halves) * LANES

    for b in range(blocks):
        for m in range(pairs):
            for h in range(2):
                for t in range(lane_tiles):
                    tiles[b * pairs + m, pl.ds(h * lane_tiles + t, 1), :] = map_ref[
                        pl.ds(others[2 * m + h], 1), pl.ds(first_col(b, t), LANES)
                    ]

    def tile_rows(t):
        for n in range(bnd // step):
            x = jnp.concatenate([halo[t, :, pl.ds(n * step, step)], pad], axis=0)
            table[pl.ds(slots + t * bnd + n * step, step), :] = dot_nt(ident, x)

    tile_rows(4)
    for piece in range(PARTS):
        arrived(0, piece)
        start(4, piece)
        start(5, piece)
        arrived(1, piece)
        start(6, piece)
        start(7, piece)
    tile_rows(1)
    tile_rows(7)
    for n in range(2, 8):
        for piece in range(PARTS):
            arrived(n, piece)
        tile_rows(sends[n][1])

    def fetch(t, s):
        return pltpu.make_async_copy(tiles.at[t], idx[s], idx_sem.at[s])

    def gather_multiply(t, s):
        m = lax.rem(t, pairs)
        keep = jnp.where(m == 0, 0.0, 1.0)
        for u in range(lane_tiles):
            sides = []
            for h in range(2):
                at = [idx[s][h * lane_tiles + u, r] for r in range(LANES)]
                eights = [
                    jnp.concatenate([table[pl.ds(a, 1), :] for a in at[r : r + 8]], axis=0)
                    for r in range(0, LANES, 8)
                ]
                sides.append(jnp.concatenate(eights, axis=0))
            g = jnp.concatenate(sides, axis=1).astype(BF16)
            cols = slice(u * LANES, (u + 1) * LANES)
            acc[:, cols] = acc[:, cols] * keep + dot_nt(wpair[m], g)

    dest = dest_ref[0]
    out_x[:, pl.ds(out_channels, 16), :] = jnp.full(
        (chunks, 16, LANES), dest.astype(F32), F32
    ).astype(BF16)

    def to_left(v):
        return pltpu.make_async_remote_copy(
            src_ref=out_x.at[v], dst_ref=in_x.at[v],
            send_sem=x_send.at[v], recv_sem=x_recv.at[v],
            device_id=left, device_id_type=MESH,
        )

    def to_down(v):
        return pltpu.make_async_remote_copy(
            src_ref=out_y.at[v], dst_ref=in_y.at[v],
            send_sem=y_send.at[v], recv_sem=y_recv.at[v],
            device_id=down, device_id_type=MESH,
        )

    def from_right(v, which):
        got = in_x[v].astype(F32)
        kind = got[out_channels : out_channels + 1]
        return jnp.where(kind == float(which), got[:out_channels], 0.0)

    def finish(t):
        b = lax.div(t, pairs)

        @pl.when(t - b * pairs == pairs - 1)
        def _():
            v = lax.div(b, halves)
            half = b - v * halves
            new = jnp.zeros((out_channels, LANES), F32)
            for u in range(lane_tiles):
                p = half * lane_tiles + u
                cols = pl.ds(pl.multiple_of(p * coarse_len + v * LANES, LANES), LANES)
                conv = acc[:, u * LANES : (u + 1) * LANES] + jnp.dot(
                    w_ref[centre], feat_ref[:, cols], preferred_element_type=F32
                )
                active = (map_ref[centre : centre + 1, cols] < slots).astype(F32)
                fine = jnp.maximum(conv * gain_ref[...] + bias_ref[...], 0.0) * active
                fine = fine.astype(BF16)
                fine_ref[:, cols] = fine
                new = new + jnp.dot(down_ref[p], fine, preferred_element_type=F32)
            part[v] = part[v] * jnp.where(half == 0, 0.0, 1.0) + new

            @pl.when(half == halves - 1)
            def _():
                out_x[v, pl.ds(0, out_channels), :] = part[v].astype(BF16)

                @pl.when(has_left)
                def _():
                    to_left(v).start()

    def onwards(v):
        @pl.when(has_right)
        def _():
            to_left(v).wait_recv()

        out_y[v] = (jnp.where(dest == 2, part[v], 0.0) + from_right(v, 3)).astype(BF16)

        @pl.when(has_down)
        def _():
            to_down(v).start()

    part[...] = jnp.zeros_like(part)
    acc[...] = jnp.zeros_like(acc)
    fetch(0, 0).start()
    fetch(1, 1).start()

    def body(n, _):
        for s in range(2):
            t = 2 * n + s
            fetch(t, s).wait()
            gather_multiply(t, s)
            fetch(jnp.minimum(t + 2, total - 1), s).start()
            finish(t)
        v = lax.div(2 * n, pairs * halves)

        @pl.when(both(v > 0, lax.div(2 * n - v * pairs * halves, 2) == pairs // 4))
        def _():
            onwards(v - 1)

        return 0

    lax.fori_loop(0, total // 2, body, 0)
    fetch(total - 1, 0).wait()
    fetch(total - 1, 1).wait()

    onwards(chunks - 1)
    for v in range(chunks):
        @pl.when(has_up)
        def _():
            to_down(v).wait_recv()

        coarse_ref[:, pl.ds(v * LANES, LANES)] = (
            jnp.where(dest == 0, part[v], 0.0) + from_right(v, 1) + in_y[v].astype(F32)
        ).astype(BF16)

    for n in range(8):
        @pl.when(sends[n][3])
        def _():
            for piece in range(PARTS):
                boundary(n, piece).wait_send()
    for v in range(chunks):
        @pl.when(has_left)
        def _():
            to_left(v).wait_send()

        @pl.when(has_down)
        def _():
            to_down(v).wait_send()


def shards(
    features, kernel_map, send_rows, conv_weight, conv_gain, conv_bias, down_weight, coarse_dest
):
    channels, slots = features.shape
    bnd = send_rows.shape[0]
    koff = kernel_map.shape[0]
    pairs = koff // 2
    total = slots // QC * pairs
    out_channels = down_weight.shape[1]
    coarse_len = slots // 8
    chunks = coarse_len // LANES
    nx, ny = lax.axis_size("gx"), lax.axis_size("gy")
    vmem = pl.BlockSpec(memory_space=pltpu.VMEM)
    smem = pl.BlockSpec(memory_space=pltpu.SMEM)

    def kernel(*refs):
        conv_kernel(nx, ny, *refs)

    fine, coarse = pl.pallas_call(
        kernel,
        in_specs=[smem] + [pl.BlockSpec(memory_space=pltpu.HBM)] * 7,
        out_specs=[vmem] * 2,
        out_shape=[
            jax.ShapeDtypeStruct((channels, slots), BF16),
            jax.ShapeDtypeStruct((out_channels, coarse_len), BF16),
        ],
        scratch_shapes=[
            pltpu.SMEM((bnd,), jnp.int32),
            pltpu.VMEM(kernel_map.shape, jnp.int32),
            pltpu.VMEM(features.shape, BF16),
            pltpu.VMEM(conv_weight.shape, BF16),
            pltpu.VMEM((1, channels), F32),
            pltpu.VMEM((1, channels), F32),
            pltpu.VMEM(down_weight.shape, BF16),
            pltpu.SemaphoreType.DMA((7,)),
            pltpu.SMEM((2 * QC // LANES, LANES), jnp.int32),
            pltpu.SMEM((2 * QC // LANES, LANES), jnp.int32),
            pltpu.VMEM((total, 2 * QC // LANES, LANES), jnp.int32),
            pltpu.VMEM((slots + 9 * bnd + 8, LANES), F32),
            pltpu.VMEM((bnd, LANES), F32),
            pltpu.VMEM((9, channels, bnd), BF16),
            pltpu.VMEM((pairs, channels, 2 * LANES), BF16),
            pltpu.VMEM((channels, QC), F32),
            pltpu.VMEM((chunks, out_channels, LANES), F32),
            pltpu.VMEM((chunks, out_channels + 16, LANES), BF16),
            pltpu.VMEM((chunks, out_channels + 16, LANES), BF16),
            pltpu.VMEM((chunks, out_channels, LANES), BF16),
            pltpu.VMEM((chunks, out_channels, LANES), BF16),
            pltpu.SemaphoreType.DMA((2,)),
            pltpu.SemaphoreType.DMA((8, PARTS)),
            pltpu.SemaphoreType.DMA((8, PARTS)),
            pltpu.SemaphoreType.DMA((chunks,)),
            pltpu.SemaphoreType.DMA((chunks,)),
            pltpu.SemaphoreType.DMA((chunks,)),
            pltpu.SemaphoreType.DMA((chunks,)),
        ]
        + [pltpu.VMEM((channels, 1), F32)] * 2,
        compiler_params=pltpu.CompilerParams(
            vmem_limit_bytes=61 * 2**20, collective_id=0, has_side_effects=True
        ),
        name="sparse_conv",
    )(
        coarse_dest, send_rows, kernel_map, features, conv_weight,
        conv_gain[None, :], conv_bias[None, :], down_weight,
    )
    return (fine, coarse)


def solution(mesh):
    placed = (
        P(None, ("gx", "gy")),
        P(None, ("gx", "gy")),
        P(("gx", "gy")),
        P(),
        P(),
        P(),
        P(),
        P(("gx", "gy")),
    )
    return jax.shard_map(
        shards,
        mesh=mesh,
        in_specs=placed,
        out_specs=(P(None, ("gx", "gy")), P(None, ("gx", "gy"))),
        check_vma=False,
    )
```

```python
import jax
import jax.numpy as jnp
from jax import lax
from jax.experimental import pallas as pl
from jax.experimental.pallas import tpu as pltpu
from jax.sharding import PartitionSpec as P

F32 = jnp.float32
BF16 = jnp.bfloat16
LANES = 128
QC = 1024
STEP = 2
PARTS = 3
MESH = pl.DeviceIdType.MESH


def dot_nt(a, b):
    return lax.dot_general(a, b, (((1,), (1,)), ((), ())), preferred_element_type=F32)


def eye(rows, cols):
    r = lax.broadcasted_iota(jnp.int32, (rows, cols), 0)
    c = lax.broadcasted_iota(jnp.int32, (rows, cols), 1)
    return (r == c).astype(BF16)


def conv_kernel(
    nx, ny,
    dest_ref, *refs,
):
    hbm, refs = refs[:7], refs[7:]
    fine_ref, coarse_ref = refs[:2]
    here, in_sem = refs[2:9], refs[9]
    compute(nx, ny, dest_ref, fine_ref, coarse_ref, hbm, here, in_sem, *refs[10:])


def compute(
    nx, ny, dest_ref, fine_ref, coarse_ref, hbm, here, in_sem,
    idx_a, idx_b, tiles, table, offered, halo, wpair, acc, part, out_x, in_x, out_y, in_y,
    idx_sem, halo_send, halo_recv, x_send, x_recv, y_send, y_recv,
    gain_ref, bias_ref,
):
    send_ref, map_ref, feat_ref, w_ref, gain_row, bias_row, down_ref = here
    send_n, map_n, feat_n, w_n, gain_n, bias_n, down_n = range(7)

    def load(n):
        return pltpu.make_async_copy(hbm[n], here[n], in_sem.at[n])

    for n in (feat_n, send_n, w_n, map_n, gain_n, bias_n, down_n):
        load(n).start()
    channels, slots = feat_ref.shape
    bnd = halo.shape[2]
    koff = map_ref.shape[0]
    centre = koff // 2
    others = [k for k in range(koff) if k != centre]
    pairs = len(others) // 2
    blocks = slots // QC
    total = blocks * pairs
    lane_tiles = QC // LANES
    coarse_len = slots // 8
    halves = 8 // lane_tiles
    chunks = blocks // halves
    out_channels = part.shape[1]
    idx = (idx_a, idx_b)

    i, j = lax.axis_index("gx"), lax.axis_index("gy")
    has_left, has_right = i > 0, i < nx - 1
    has_down, has_up = j > 0, j < ny - 1
    around = (
        (has_left, (i - 1, j)),
        (has_right, (i + 1, j)),
        (has_down, (i, j - 1)),
        (has_up, (i, j + 1)),
    )

    both = jnp.logical_and
    inner = both(both(has_left, has_right), both(has_down, has_up))

    @pl.when(jnp.logical_not(inner))
    def _():
        halo[...] = jnp.zeros_like(halo)
        in_x[...] = jnp.zeros_like(in_x)
        in_y[...] = jnp.zeros_like(in_y)

    barrier = pltpu.get_barrier_semaphore()
    for there, device in around:
        @pl.when(there)
        def _():
            pl.semaphore_signal(barrier, inc=1, device_id=device, device_id_type=MESH)

    step = 256
    ident = eye(step, step)
    pad = jnp.zeros((LANES - channels, step), BF16)

    def own_rows(n, _):
        c0 = pl.multiple_of(n * step, step)
        x = jnp.concatenate([feat_ref[:, pl.ds(c0, step)], pad], axis=0)
        table[pl.ds(c0, step), :] = dot_nt(ident, x)
        return 0

    load(feat_n).wait()
    lax.fori_loop(0, slots // step, own_rows, 0, unroll=8)
    table[pl.ds(slots + 9 * bnd, 8), :] = jnp.zeros((8, LANES), F32)

    load(send_n).wait()
    for r in range(bnd):
        offered[pl.ds(r, 1), :] = table[pl.ds(send_ref[r], 1), :]
    halo[4] = dot_nt(eye(channels, LANES), offered[...].astype(BF16)).astype(BF16)

    pl.semaphore_wait(barrier, sum(there.astype(jnp.int32) for there, _ in around))

    right, left, up, down = (i + 1, j), (i - 1, j), (i, j + 1), (i, j - 1)
    sends = (
        (4, 1, right, has_right, has_left),
        (4, 7, left, has_left, has_right),
        (4, 3, up, has_up, has_down),
        (4, 5, down, has_down, has_up),
        (1, 0, up, both(has_left, has_up), both(has_left, has_down)),
        (1, 2, down, both(has_left, has_down), both(has_left, has_up)),
        (7, 6, up, both(has_right, has_up), both(has_right, has_down)),
        (7, 8, down, both(has_right, has_down), both(has_right, has_up)),
    )
    depth = channels // PARTS

    def boundary(n, piece):
        src, dst, device, _, _ = sends[n]
        span = pl.ds(piece * depth, depth)
        return pltpu.make_async_remote_copy(
            src_ref=halo.at[src, span],
            dst_ref=halo.at[dst, span],
            send_sem=halo_send.at[n, piece],
            recv_sem=halo_recv.at[n, piece],
            device_id=device,
            device_id_type=MESH,
        )

    def start(n, piece):
        @pl.when(sends[n][3])
        def _():
            boundary(n, piece).start()

    def arrived(n, piece):
        @pl.when(sends[n][4])
        def _():
            boundary(n, piece).wait_recv()

    for piece in range(PARTS):
        for n in range(4):
            start(n, piece)

    load(w_n).wait()
    wpair[...] = jnp.zeros_like(wpair)
    for n, k in enumerate(others):
        wpair[n // 2, :, pl.ds((n % 2) * LANES, channels)] = w_ref[k]

    load(gain_n).wait()
    load(bias_n).wait()
    for row, column in ((gain_row, gain_ref), (bias_row, bias_ref)):
        spread = jnp.where(eye(channels, channels) > 0, row[...], 0.0)
        column[...] = jnp.sum(spread, axis=1, keepdims=True)
    load(down_n).wait()
    load(map_n).wait()

    def first_col(b, t):
        return ((b % halves) * lane_tiles + t) * coarse_len + (b // halves) * LANES

    for b in range(blocks):
        for m in range(pairs):
            for h in range(2):
                for t in range(lane_tiles):
                    tiles[
                        (b * pairs + m) // STEP,
                        pl.ds((b * pairs + m) % STEP * 2 * lane_tiles + h * lane_tiles + t, 1),
                        :,
                    ] = map_ref[
                        pl.ds(others[2 * m + h], 1), pl.ds(first_col(b, t), LANES)
                    ]

    def tile_rows(t):
        for n in range(bnd // step):
            x = jnp.concatenate([halo[t, :, pl.ds(n * step, step)], pad], axis=0)
            table[pl.ds(slots + t * bnd + n * step, step), :] = dot_nt(ident, x)

    tile_rows(4)
    for piece in range(PARTS):
        arrived(0, piece)
        start(4, piece)
        start(5, piece)
        arrived(1, piece)
        start(6, piece)
        start(7, piece)
    tile_rows(1)
    tile_rows(7)
    for n in range(2, 8):
        for piece in range(PARTS):
            arrived(n, piece)
        tile_rows(sends[n][1])

    def fetch(t, s):
        return pltpu.make_async_copy(tiles.at[t], idx[s], idx_sem.at[s])

    def gather_multiply(t, s, e):
        b = lax.div(t, pairs)
        m = t - b * pairs
        keep = jnp.where(m == 0, 0.0, 1.0)
        first = e * 2 * lane_tiles
        for u in range(lane_tiles):
            sides = []
            for h in range(2):
                at = [idx[s][first + h * lane_tiles + u, r] for r in range(LANES)]
                eights = [
                    jnp.concatenate([table[pl.ds(a, 1), :] for a in at[r : r + 8]], axis=0)
                    for r in range(0, LANES, 8)
                ]
                sides.append(jnp.concatenate(eights, axis=0))
            g = jnp.concatenate(sides, axis=1).astype(BF16)
            cols = slice(u * LANES, (u + 1) * LANES)
            acc[b, :, cols] = acc[b, :, cols] * keep + dot_nt(wpair[m], g)

    dest = dest_ref[0]
    out_x[:, pl.ds(out_channels, 16), :] = jnp.full(
        (chunks, 16, LANES), dest.astype(F32), F32
    ).astype(BF16)

    def to_left(v):
        return pltpu.make_async_remote_copy(
            src_ref=out_x.at[v], dst_ref=in_x.at[v],
            send_sem=x_send.at[v], recv_sem=x_recv.at[v],
            device_id=left, device_id_type=MESH,
        )

    def to_down(v):
        return pltpu.make_async_remote_copy(
            src_ref=out_y.at[v], dst_ref=in_y.at[v],
            send_sem=y_send.at[v], recv_sem=y_recv.at[v],
            device_id=down, device_id_type=MESH,
        )

    def from_right(v, which):
        got = in_x[v].astype(F32)
        kind = got[out_channels : out_channels + 1]
        return jnp.where(kind == float(which), got[:out_channels], 0.0)

    def finish(t):
        b = lax.div(t, pairs)

        @pl.when(t - b * pairs == pairs - 1)
        def _():
            v = lax.div(b, halves)
            half = b - v * halves
            new = jnp.zeros((out_channels, LANES), F32)
            for u in range(lane_tiles):
                p = half * lane_tiles + u
                cols = pl.ds(pl.multiple_of(p * coarse_len + v * LANES, LANES), LANES)
                conv = acc[b, :, u * LANES : (u + 1) * LANES] + jnp.dot(
                    w_ref[centre], feat_ref[:, cols], preferred_element_type=F32
                )
                active = (map_ref[centre : centre + 1, cols] < slots).astype(F32)
                fine = jnp.maximum(conv * gain_ref[...] + bias_ref[...], 0.0) * active
                fine = fine.astype(BF16)
                fine_ref[:, cols] = fine
                new = new + jnp.dot(down_ref[p], fine, preferred_element_type=F32)
            part[v] = part[v] * jnp.where(half == 0, 0.0, 1.0) + new

            @pl.when(half == halves - 1)
            def _():
                out_x[v, pl.ds(0, out_channels), :] = part[v].astype(BF16)

                @pl.when(has_left)
                def _():
                    to_left(v).start()

    def onwards(v):
        @pl.when(has_right)
        def _():
            to_left(v).wait_recv()

        out_y[v] = (jnp.where(dest == 2, part[v], 0.0) + from_right(v, 3)).astype(BF16)

        @pl.when(has_down)
        def _():
            to_down(v).start()

    part[...] = jnp.zeros_like(part)
    acc[...] = jnp.zeros_like(acc)
    fetch(0, 0).start()
    fetch(1, 1).start()

    steps = total // STEP

    def body(n, _):
        for s in range(2):
            step_now = 2 * n + s
            fetch(step_now, s).wait()
            for e in range(STEP):
                gather_multiply(step_now * STEP + e, s, e)
            fetch(jnp.minimum(step_now + 2, steps - 1), s).start()
            for e in range(STEP):
                finish(step_now * STEP + e)
        t = 2 * STEP * n
        v = lax.div(t, pairs * halves)
        since = t - v * pairs * halves

        @pl.when(both(v > 0, both(since >= 6, since < 6 + 2 * STEP)))
        def _():
            onwards(v - 1)

        return 0

    lax.fori_loop(0, steps // 2, body, 0)
    fetch(steps - 1, 0).wait()
    fetch(steps - 1, 1).wait()

    onwards(chunks - 1)
    for v in range(chunks):
        @pl.when(has_up)
        def _():
            to_down(v).wait_recv()

        coarse_ref[:, pl.ds(v * LANES, LANES)] = (
            jnp.where(dest == 0, part[v], 0.0) + from_right(v, 1) + in_y[v].astype(F32)
        ).astype(BF16)

    for n in range(8):
        @pl.when(sends[n][3])
        def _():
            for piece in range(PARTS):
                boundary(n, piece).wait_send()
    for v in range(chunks):
        @pl.when(has_left)
        def _():
            to_left(v).wait_send()

        @pl.when(has_down)
        def _():
            to_down(v).wait_send()


def shards(
    features, kernel_map, send_rows, conv_weight, conv_gain, conv_bias, down_weight, coarse_dest
):
    channels, slots = features.shape
    bnd = send_rows.shape[0]
    koff = kernel_map.shape[0]
    pairs = koff // 2
    total = slots // QC * pairs
    out_channels = down_weight.shape[1]
    coarse_len = slots // 8
    chunks = coarse_len // LANES
    nx, ny = lax.axis_size("gx"), lax.axis_size("gy")
    vmem = pl.BlockSpec(memory_space=pltpu.VMEM)
    smem = pl.BlockSpec(memory_space=pltpu.SMEM)

    def kernel(*refs):
        conv_kernel(nx, ny, *refs)

    fine, coarse = pl.pallas_call(
        kernel,
        in_specs=[smem] + [pl.BlockSpec(memory_space=pltpu.HBM)] * 7,
        out_specs=[vmem] * 2,
        out_shape=[
            jax.ShapeDtypeStruct((channels, slots), BF16),
            jax.ShapeDtypeStruct((out_channels, coarse_len), BF16),
        ],
        scratch_shapes=[
            pltpu.SMEM((bnd,), jnp.int32),
            pltpu.VMEM(kernel_map.shape, jnp.int32),
            pltpu.VMEM(features.shape, BF16),
            pltpu.VMEM(conv_weight.shape, BF16),
            pltpu.VMEM((1, channels), F32),
            pltpu.VMEM((1, channels), F32),
            pltpu.VMEM(down_weight.shape, BF16),
            pltpu.SemaphoreType.DMA((7,)),
            pltpu.SMEM((STEP * 2 * QC // LANES, LANES), jnp.int32),
            pltpu.SMEM((STEP * 2 * QC // LANES, LANES), jnp.int32),
            pltpu.VMEM((total // STEP, STEP * 2 * QC // LANES, LANES), jnp.int32),
            pltpu.VMEM((slots + 9 * bnd + 8, LANES), F32),
            pltpu.VMEM((bnd, LANES), F32),
            pltpu.VMEM((9, channels, bnd), BF16),
            pltpu.VMEM((pairs, channels, 2 * LANES), BF16),
            pltpu.VMEM((slots // QC, channels, QC), F32),
            pltpu.VMEM((chunks, out_channels, LANES), F32),
            pltpu.VMEM((chunks, out_channels + 16, LANES), BF16),
            pltpu.VMEM((chunks, out_channels + 16, LANES), BF16),
            pltpu.VMEM((chunks, out_channels, LANES), BF16),
            pltpu.VMEM((chunks, out_channels, LANES), BF16),
            pltpu.SemaphoreType.DMA((2,)),
            pltpu.SemaphoreType.DMA((8, PARTS)),
            pltpu.SemaphoreType.DMA((8, PARTS)),
            pltpu.SemaphoreType.DMA((chunks,)),
            pltpu.SemaphoreType.DMA((chunks,)),
            pltpu.SemaphoreType.DMA((chunks,)),
            pltpu.SemaphoreType.DMA((chunks,)),
        ]
        + [pltpu.VMEM((channels, 1), F32)] * 2,
        compiler_params=pltpu.CompilerParams(
            vmem_limit_bytes=61 * 2**20, collective_id=0, has_side_effects=True
        ),
        name="sparse_conv",
    )(
        coarse_dest, send_rows, kernel_map, features, conv_weight,
        conv_gain[None, :], conv_bias[None, :], down_weight,
    )
    return (fine, coarse)


def solution(mesh):
    placed = (
        P(None, ("gx", "gy")),
        P(None, ("gx", "gy")),
        P(("gx", "gy")),
        P(),
        P(),
        P(),
        P(),
        P(("gx", "gy")),
    )
    return jax.shard_map(
        shards,
        mesh=mesh,
        in_specs=placed,
        out_specs=(P(None, ("gx", "gy")), P(None, ("gx", "gy"))),
        check_vma=False,
    )
```

```python
import jax
import jax.numpy as jnp
from jax import lax
from jax.experimental import pallas as pl
from jax.experimental.pallas import tpu as pltpu
from jax.sharding import PartitionSpec as P

F32 = jnp.float32
BF16 = jnp.bfloat16
LANES = 128
QC = 1024
STEP = 2
WIDE = 2
PARTS = 3
MESH = pl.DeviceIdType.MESH


def dot_nt(a, b):
    return lax.dot_general(a, b, (((1,), (1,)), ((), ())), preferred_element_type=F32)


def eye(rows, cols):
    r = lax.broadcasted_iota(jnp.int32, (rows, cols), 0)
    c = lax.broadcasted_iota(jnp.int32, (rows, cols), 1)
    return (r == c).astype(BF16)


def conv_kernel(
    nx, ny,
    dest_ref, *refs,
):
    hbm, refs = refs[:7], refs[7:]
    fine_ref, coarse_ref = refs[:2]
    here, in_sem = refs[2:9], refs[9]
    fine_here, fine_sem = refs[10:12]
    fine_copy = pltpu.make_async_copy(fine_here, fine_ref, fine_sem)
    compute(nx, ny, dest_ref, fine_here, coarse_ref, fine_copy, hbm, here, in_sem, *refs[12:])
    fine_copy.wait()


def compute(
    nx, ny, dest_ref, fine_ref, coarse_ref, fine_copy, hbm, here, in_sem,
    idx_a, idx_b, tiles, table, offered, halo, wpair, acc, part, out_x, in_x, out_y, in_y,
    idx_sem, halo_send, halo_recv, x_send, x_recv, y_send, y_recv,
    gain_ref, bias_ref,
):
    send_ref, map_ref, feat_ref, w_ref, gain_row, bias_row, down_ref = here
    send_n, map_n, feat_n, w_n, gain_n, bias_n, down_n = range(7)

    def load(n):
        return pltpu.make_async_copy(hbm[n], here[n], in_sem.at[n])

    for n in (feat_n, send_n, w_n, map_n, gain_n, bias_n, down_n):
        load(n).start()
    channels, slots = feat_ref.shape
    bnd = halo.shape[2]
    koff = map_ref.shape[0]
    centre = koff // 2
    others = [k for k in range(koff) if k != centre]
    pairs = len(others) // 2
    blocks = slots // QC
    total = blocks * pairs
    lane_tiles = QC // LANES
    coarse_len = slots // 8
    halves = 8 // lane_tiles
    chunks = blocks // halves
    out_channels = part.shape[1]
    idx = (idx_a, idx_b)

    i, j = lax.axis_index("gx"), lax.axis_index("gy")
    has_left, has_right = i > 0, i < nx - 1
    has_down, has_up = j > 0, j < ny - 1
    around = (
        (has_left, (i - 1, j)),
        (has_right, (i + 1, j)),
        (has_down, (i, j - 1)),
        (has_up, (i, j + 1)),
    )

    both = jnp.logical_and
    inner = both(both(has_left, has_right), both(has_down, has_up))

    @pl.when(jnp.logical_not(inner))
    def _():
        halo[...] = jnp.zeros_like(halo)
        in_x[...] = jnp.zeros_like(in_x)
        in_y[...] = jnp.zeros_like(in_y)

    barrier = pltpu.get_barrier_semaphore()
    for there, device in around:
        @pl.when(there)
        def _():
            pl.semaphore_signal(barrier, inc=1, device_id=device, device_id_type=MESH)

    step = 256
    ident = eye(step, step)
    pad = jnp.zeros((LANES - channels, step), BF16)

    def own_rows(n, _):
        c0 = pl.multiple_of(n * step, step)
        x = jnp.concatenate([feat_ref[:, pl.ds(c0, step)], pad], axis=0)
        table[pl.ds(c0, step), :] = dot_nt(ident, x)
        return 0

    load(feat_n).wait()
    lax.fori_loop(0, slots // step, own_rows, 0, unroll=8)
    table[pl.ds(slots + 9 * bnd, 8), :] = jnp.zeros((8, LANES), F32)

    load(send_n).wait()
    for r in range(bnd):
        offered[pl.ds(r, 1), :] = table[pl.ds(send_ref[r], 1), :]
    halo[4] = dot_nt(eye(channels, LANES), offered[...].astype(BF16)).astype(BF16)

    pl.semaphore_wait(barrier, sum(there.astype(jnp.int32) for there, _ in around))

    right, left, up, down = (i + 1, j), (i - 1, j), (i, j + 1), (i, j - 1)
    sends = (
        (4, 1, right, has_right, has_left),
        (4, 7, left, has_left, has_right),
        (4, 3, up, has_up, has_down),
        (4, 5, down, has_down, has_up),
        (1, 0, up, both(has_left, has_up), both(has_left, has_down)),
        (1, 2, down, both(has_left, has_down), both(has_left, has_up)),
        (7, 6, up, both(has_right, has_up), both(has_right, has_down)),
        (7, 8, down, both(has_right, has_down), both(has_right, has_up)),
    )
    depth = channels // PARTS

    def boundary(n, piece):
        src, dst, device, _, _ = sends[n]
        span = pl.ds(piece * depth, depth)
        return pltpu.make_async_remote_copy(
            src_ref=halo.at[src, span],
            dst_ref=halo.at[dst, span],
            send_sem=halo_send.at[n, piece],
            recv_sem=halo_recv.at[n, piece],
            device_id=device,
            device_id_type=MESH,
        )

    def start(n, piece):
        @pl.when(sends[n][3])
        def _():
            boundary(n, piece).start()

    def arrived(n, piece):
        @pl.when(sends[n][4])
        def _():
            boundary(n, piece).wait_recv()

    for piece in range(PARTS):
        for n in range(4):
            start(n, piece)

    load(w_n).wait()
    wpair[...] = jnp.zeros_like(wpair)
    for n, k in enumerate(others):
        wpair[n // 2, :, pl.ds((n % 2) * LANES, channels)] = w_ref[k]

    load(gain_n).wait()
    load(bias_n).wait()
    for row, column in ((gain_row, gain_ref), (bias_row, bias_ref)):
        spread = jnp.where(eye(channels, channels) > 0, row[...], 0.0)
        column[...] = jnp.sum(spread, axis=1, keepdims=True)
    load(down_n).wait()
    load(map_n).wait()

    def first_col(b, t):
        return ((b % halves) * lane_tiles + t) * coarse_len + (b // halves) * LANES

    for b in range(blocks):
        for m in range(pairs):
            for h in range(2):
                for t in range(lane_tiles):
                    tiles[
                        (b * pairs + m) // STEP,
                        pl.ds((b * pairs + m) % STEP * 2 * lane_tiles + h * lane_tiles + t, 1),
                        :,
                    ] = map_ref[
                        pl.ds(others[2 * m + h], 1), pl.ds(first_col(b, t), LANES)
                    ]

    def tile_rows(t):
        for n in range(bnd // step):
            x = jnp.concatenate([halo[t, :, pl.ds(n * step, step)], pad], axis=0)
            table[pl.ds(slots + t * bnd + n * step, step), :] = dot_nt(ident, x)

    for b in range(blocks):
        own = [feat_ref[:, pl.ds(first_col(b, t), LANES)] for t in range(lane_tiles)]
        acc[b] = jnp.dot(
            w_ref[centre], jnp.concatenate(own, axis=1), preferred_element_type=F32
        )

    tile_rows(4)
    for piece in range(PARTS):
        arrived(0, piece)
        start(4, piece)
        start(5, piece)
        arrived(1, piece)
        start(6, piece)
        start(7, piece)
    tile_rows(1)
    tile_rows(7)
    for n in range(2, 8):
        for piece in range(PARTS):
            arrived(n, piece)
        tile_rows(sends[n][1])

    def fetch(t, s):
        return pltpu.make_async_copy(tiles.at[t], idx[s], idx_sem.at[s])

    def gather_multiply(t, s, e):
        b = lax.div(t, pairs)
        m = t - b * pairs
        first = e * 2 * lane_tiles
        for u in range(0, lane_tiles, WIDE):
            sides = []
            for h in range(2):
                at = [
                    idx[s][first + h * lane_tiles + u + w, r]
                    for w in range(WIDE)
                    for r in range(LANES)
                ]
                eights = [
                    jnp.concatenate([table[pl.ds(a, 1), :] for a in at[r : r + 8]], axis=0)
                    for r in range(0, WIDE * LANES, 8)
                ]
                sides.append(jnp.concatenate(eights, axis=0))
            g = jnp.concatenate(sides, axis=1).astype(BF16)
            cols = slice(u * LANES, (u + WIDE) * LANES)
            acc[b, :, cols] = acc[b, :, cols] + dot_nt(wpair[m], g)

    dest = dest_ref[0]
    out_x[:, pl.ds(out_channels, 16), :] = jnp.full(
        (chunks, 16, LANES), dest.astype(F32), F32
    ).astype(BF16)

    def to_left(v):
        return pltpu.make_async_remote_copy(
            src_ref=out_x.at[v], dst_ref=in_x.at[v],
            send_sem=x_send.at[v], recv_sem=x_recv.at[v],
            device_id=left, device_id_type=MESH,
        )

    def to_down(v):
        return pltpu.make_async_remote_copy(
            src_ref=out_y.at[v], dst_ref=in_y.at[v],
            send_sem=y_send.at[v], recv_sem=y_recv.at[v],
            device_id=down, device_id_type=MESH,
        )

    def from_right(v, which):
        got = in_x[v].astype(F32)
        kind = got[out_channels : out_channels + 1]
        return jnp.where(kind == float(which), got[:out_channels], 0.0)

    def finish(t):
        b = lax.div(t, pairs)

        @pl.when(t - b * pairs == pairs - 1)
        def _():
            v = lax.div(b, halves)
            half = b - v * halves
            new = jnp.zeros((out_channels, LANES), F32)
            for u in range(lane_tiles):
                p = half * lane_tiles + u
                cols = pl.ds(pl.multiple_of(p * coarse_len + v * LANES, LANES), LANES)
                conv = acc[b, :, u * LANES : (u + 1) * LANES]
                active = (map_ref[centre : centre + 1, cols] < slots).astype(F32)
                fine = jnp.maximum(conv * gain_ref[...] + bias_ref[...], 0.0) * active
                fine = fine.astype(BF16)
                fine_ref[:, cols] = fine
                new = new + jnp.dot(down_ref[p], fine, preferred_element_type=F32)
            part[v] = part[v] * jnp.where(half == 0, 0.0, 1.0) + new

            @pl.when(half == halves - 1)
            def _():
                out_x[v, pl.ds(0, out_channels), :] = part[v].astype(BF16)

                @pl.when(has_left)
                def _():
                    to_left(v).start()

    def onwards(v):
        @pl.when(has_right)
        def _():
            to_left(v).wait_recv()

        out_y[v] = (jnp.where(dest == 2, part[v], 0.0) + from_right(v, 3)).astype(BF16)

        @pl.when(has_down)
        def _():
            to_down(v).start()

    part[...] = jnp.zeros_like(part)
    fetch(0, 0).start()
    fetch(1, 1).start()

    steps = total // STEP

    def body(n, _):
        for s in range(2):
            step_now = 2 * n + s
            fetch(step_now, s).wait()
            for e in range(STEP):
                gather_multiply(step_now * STEP + e, s, e)
            fetch(jnp.minimum(step_now + 2, steps - 1), s).start()
            for e in range(STEP):
                finish(step_now * STEP + e)
        t = 2 * STEP * n
        v = lax.div(t, pairs * halves)
        since = t - v * pairs * halves

        @pl.when(both(v > 0, both(since >= 6, since < 6 + 2 * STEP)))
        def _():
            onwards(v - 1)

        return 0

    lax.fori_loop(0, steps // 2, body, 0)
    fetch(steps - 1, 0).wait()
    fetch(steps - 1, 1).wait()

    fine_copy.start()
    onwards(chunks - 1)
    for v in range(chunks):
        @pl.when(has_up)
        def _():
            to_down(v).wait_recv()

        coarse_ref[:, pl.ds(v * LANES, LANES)] = (
            jnp.where(dest == 0, part[v], 0.0) + from_right(v, 1) + in_y[v].astype(F32)
        ).astype(BF16)

    for n in range(8):
        @pl.when(sends[n][3])
        def _():
            for piece in range(PARTS):
                boundary(n, piece).wait_send()
    for v in range(chunks):
        @pl.when(has_left)
        def _():
            to_left(v).wait_send()

        @pl.when(has_down)
        def _():
            to_down(v).wait_send()


def shards(
    features, kernel_map, send_rows, conv_weight, conv_gain, conv_bias, down_weight, coarse_dest
):
    channels, slots = features.shape
    bnd = send_rows.shape[0]
    koff = kernel_map.shape[0]
    pairs = koff // 2
    total = slots // QC * pairs
    out_channels = down_weight.shape[1]
    coarse_len = slots // 8
    chunks = coarse_len // LANES
    nx, ny = lax.axis_size("gx"), lax.axis_size("gy")
    vmem = pl.BlockSpec(memory_space=pltpu.VMEM)
    smem = pl.BlockSpec(memory_space=pltpu.SMEM)

    def kernel(*refs):
        conv_kernel(nx, ny, *refs)

    fine, coarse = pl.pallas_call(
        kernel,
        in_specs=[smem] + [pl.BlockSpec(memory_space=pltpu.HBM)] * 7,
        out_specs=[pl.BlockSpec(memory_space=pltpu.HBM), vmem],
        out_shape=[
            jax.ShapeDtypeStruct((channels, slots), BF16),
            jax.ShapeDtypeStruct((out_channels, coarse_len), BF16),
        ],
        scratch_shapes=[
            pltpu.SMEM((bnd,), jnp.int32),
            pltpu.VMEM(kernel_map.shape, jnp.int32),
            pltpu.VMEM(features.shape, BF16),
            pltpu.VMEM(conv_weight.shape, BF16),
            pltpu.VMEM((1, channels), F32),
            pltpu.VMEM((1, channels), F32),
            pltpu.VMEM(down_weight.shape, BF16),
            pltpu.SemaphoreType.DMA((7,)),
            pltpu.VMEM(features.shape, BF16),
            pltpu.SemaphoreType.DMA,
            pltpu.SMEM((STEP * 2 * QC // LANES, LANES), jnp.int32),
            pltpu.SMEM((STEP * 2 * QC // LANES, LANES), jnp.int32),
            pltpu.VMEM((total // STEP, STEP * 2 * QC // LANES, LANES), jnp.int32),
            pltpu.VMEM((slots + 9 * bnd + 8, LANES), F32),
            pltpu.VMEM((bnd, LANES), F32),
            pltpu.VMEM((9, channels, bnd), BF16),
            pltpu.VMEM((pairs, channels, 2 * LANES), BF16),
            pltpu.VMEM((slots // QC, channels, QC), F32),
            pltpu.VMEM((chunks, out_channels, LANES), F32),
            pltpu.VMEM((chunks, out_channels + 16, LANES), BF16),
            pltpu.VMEM((chunks, out_channels + 16, LANES), BF16),
            pltpu.VMEM((chunks, out_channels, LANES), BF16),
            pltpu.VMEM((chunks, out_channels, LANES), BF16),
            pltpu.SemaphoreType.DMA((2,)),
            pltpu.SemaphoreType.DMA((8, PARTS)),
            pltpu.SemaphoreType.DMA((8, PARTS)),
            pltpu.SemaphoreType.DMA((chunks,)),
            pltpu.SemaphoreType.DMA((chunks,)),
            pltpu.SemaphoreType.DMA((chunks,)),
            pltpu.SemaphoreType.DMA((chunks,)),
        ]
        + [pltpu.VMEM((channels, 1), F32)] * 2,
        compiler_params=pltpu.CompilerParams(
            vmem_limit_bytes=61 * 2**20, collective_id=0, has_side_effects=True
        ),
        name="sparse_conv",
    )(
        coarse_dest, send_rows, kernel_map, features, conv_weight,
        conv_gain[None, :], conv_bias[None, :], down_weight,
    )
    return (fine, coarse)


def solution(mesh):
    placed = (
        P(None, ("gx", "gy")),
        P(None, ("gx", "gy")),
        P(("gx", "gy")),
        P(),
        P(),
        P(),
        P(),
        P(("gx", "gy")),
    )
    return jax.shard_map(
        shards,
        mesh=mesh,
        in_specs=placed,
        out_specs=(P(None, ("gx", "gy")), P(None, ("gx", "gy"))),
        check_vma=False,
    )
```
